32 devices in a mesh: groups: 2 (over y), vocab: 4 (over z), tokens: 2 (over x), sub: 2 (over core).
Axes of the slice: x: 2, y: 2, z: 4, core: 2. Of those that a mesh axis runs over, the one named last changes fastest.
Arguments:
- student_hidden: bfloat16 [256, 4096], P(('groups', 'tokens', 'sub'), 'vocab'), parts along dimension 0, may hold values from -32 to 32
- teacher_hidden: bfloat16 [512, 4096], P(('groups', 'tokens', 'sub'), 'vocab'), parts along dimension 0, may hold values from -32 to 32
- student_head: bfloat16 [4992, 4096], P(('vocab', 'tokens', 'sub')), may hold values from -0.28125 to 0.28125
- teacher_head: bfloat16 [4992, 4096], P(('vocab', 'tokens', 'sub')), may hold values from -0.28125 to 0.28125
- token_ids: int32 [256], P('groups'), parts along dimension 0, may hold values from 0 to 4991
- requests: int32 [8, 4, 16], P('groups'), parts along dimension 0, may hold values from 0 to 63, as said below
- counts: int32 [8, 4], P('groups'), parts along dimension 0, may hold values from 0 to 16, as said below
- kl_weights: float32 [256], P('groups'), parts along dimension 0, may hold values from 0.5 to 2
Outputs:
- grad_hidden: float32 [256, 4096], P(('groups', 'tokens', 'sub'), 'vocab'), parts along dimension 0
- kl: float32 [256], P(('groups', 'tokens', 'sub')), parts along dimension 0
- log_ratio: float32 [256], P(('groups', 'tokens', 'sub')), parts along dimension 0
The draws below stay inside these ranges and needn't reach their ends.
There are 2 independent parts, one for each index of `groups`. The reference program is written for one: setup_inputs(seed, part) draws one part's arguments, and reference() takes and returns one part's arrays. A program takes and returns all parts, laid end to end along the dimension named above; an argument that names none is the same for every part. Nothing has to cross between parts.
Inputs may be any that keep to these rules, and one draw needn't show every extreme that they name: `counts`: row o lists how many of owner o's 32 rows each serving shard supplies, in shard order; each row sums to 32, and in each row one shard supplies exactly 16. requests[o, j, k] for k < counts[o, j] is a row local to serving shard j; over all owners no row of a shard is requested twice; later slots hold valid rows that are not used.
All inputs are finite; a program needn't handle non-finite values.
Results may differ from the reference program's by a relative error of at most 0.012.
Values may be sent and summed in bfloat16 or wider, within the bound.
A program may use at most 64 MiB of HBM per device.

```python
import math
import jax
import jax.numpy as jnp
import numpy as np
from jax import lax

D = 4096
VOC_DEV = 312
ROW_DEV = 32
CAP = 16
OWNERS = 4
ROWS = 128
SERVE_DEV = 64
SERVE = 256
VOCAB = 4992


def drawn_rows(key, row_total):
    return jax.random.truncated_normal(key, -4.0, 4.0, (row_total, D), jnp.float32)


def route_tables(key):
    keys = jax.random.split(key, 3)
    shards = jnp.arange(OWNERS, dtype=jnp.int32)
    largest = jax.random.randint(keys[0], (OWNERS,), 0, OWNERS)
    extra = jax.random.randint(keys[1], (OWNERS, CAP), 0, OWNERS - 1)
    extra = extra + (extra >= largest[:, None]).astype(jnp.int32)
    counts = CAP * (largest[:, None] == shards[None, :]).astype(jnp.int32)
    counts = counts + jnp.sum((extra[:, :, None] == shards[None, None, :]).astype(jnp.int32), axis=1)
    counts = counts.astype(jnp.int32)
    orders = jax.vmap(lambda sub_key: jax.random.permutation(sub_key, SERVE_DEV))(jax.random.split(keys[2], OWNERS))
    orders = orders.astype(jnp.int32)
    offsets = (jnp.cumsum(counts, axis=0) - counts).astype(jnp.int32)
    slots = jnp.arange(CAP, dtype=jnp.int32)
    position = (offsets[:, :, None] + slots[None, None, :]) % SERVE_DEV
    requests = orders[shards[None, :, None], position]
    return (counts, requests.astype(jnp.int32))


def draw_counts(key, part):
    counts, requests = route_tables(key)
    return counts


def draw_requests(key, part):
    counts, requests = route_tables(key)
    return requests


def draw_student_hidden(key, part):
    key = jax.random.fold_in(key, 11)
    values = drawn_rows(key, ROWS)
    return values.astype(jnp.bfloat16)


def draw_teacher_hidden(key, part):
    key = jax.random.fold_in(key, 23)
    values = drawn_rows(key, SERVE)
    return values.astype(jnp.bfloat16)


def touch_ends(entries, key, smallest, high):
    shape = entries.shape
    index_at = [jax.random.randint(jax.random.fold_in(key, axis), (), 0, shape[axis]) for axis in range(len(shape))]
    entries = entries.at[tuple(index_at)].set(smallest)
    longest = shape.index(max(shape))
    index_at[longest] = (index_at[longest] + 1) % shape[longest]
    return entries.at[tuple(index_at)].set(high)


def shard_levels(stream_key, shape, pieces, low, top_value):
    def one(axis_at, shards_of):
        heights = jax.random.uniform(jax.random.fold_in(jax.random.fold_in(stream_key, 6), axis_at), (shards_of,), jnp.float32, low / len(pieces), top_value / len(pieces))
        return jnp.repeat(jnp.exp(heights), shape[axis_at] // shards_of).reshape((-1,) + (1,) * (len(shape) - axis_at - 1))

    loudness = one(*pieces[0])
    for cut in pieces[1:]:
        loudness = loudness * one(*cut)
    return loudness


def cumulative_ranks(count, skew):
    weights = [(1 << 20) // math.isqrt(rank ** skew) + 1 for rank in range(1, count + 1)]
    scale = 1 + sum(weights) // (1 << 30)
    return np.cumsum(np.array([max(1, weight // scale) for weight in weights]))


def ranked_ids(rng, dims, count, lean):
    table = cumulative_ranks(count, lean)
    ticket = jax.random.randint(jax.random.fold_in(rng, 1), dims, 0, int(table[count - 1]))
    standing = jnp.searchsorted(jnp.asarray(table, jnp.int32), ticket, side="right")
    return jax.random.permutation(jax.random.fold_in(rng, 2), count)[standing].astype(jnp.int32)


def scatter_about(stream_key, extent, deviation, most, cuts=(), kind=jnp.bfloat16):
    array = jax.random.normal(stream_key, extent, jnp.float32) * deviation
    if len(cuts) > 0:
        array = shard_levels(stream_key, extent, cuts, -0.22, 0.18) * array
    return jnp.clip(array, min=-most, max=most).astype(kind)


def setup_inputs(seed: int = 0, part: int = 0) -> dict:
    key_list = jax.random.split(jax.random.key(seed), 9)
    part_keys = jax.random.split(jax.random.fold_in(key_list[8], part), 9)
    return {
        "student_hidden": draw_student_hidden(jax.random.fold_in(jax.random.fold_in(key_list[8], part), 71), part),
        "teacher_hidden": draw_teacher_hidden(jax.random.fold_in(jax.random.fold_in(key_list[8], part), 71), part),
        "student_head": scatter_about(key_list[2], (VOCAB, D), (3.0 * D ** -0.5), 0.28125, ((0, 16),)),
        "teacher_head": scatter_about(key_list[3], (VOCAB, D), (3.0 * D ** -0.5), 0.28125, ((0, 16),)),
        "token_ids": touch_ends(ranked_ids(part_keys[4], (ROWS,), VOCAB, 2), jax.random.fold_in(part_keys[4], 3), 0, VOCAB - 1).astype(jnp.int32),
        "requests": draw_requests(jax.random.fold_in(jax.random.fold_in(key_list[8], part), 71), part),
        "counts": draw_counts(jax.random.fold_in(jax.random.fold_in(key_list[8], part), 71), part),
        "kl_weights": jnp.clip(jnp.exp(jax.random.uniform(part_keys[7], (ROWS,), jnp.float32, math.log(0.5), math.log(2.0))), 0.5, 2.0),
    }


def owner_layout(counts):
    starts = (jnp.cumsum(counts, axis=1) - counts).astype(jnp.int32)
    within = jnp.arange(ROW_DEV, dtype=jnp.int32)
    source = (jnp.sum((starts[:, None, :] <= within[None, :, None]).astype(jnp.int32), axis=2) - 1).astype(jnp.int32)
    slot_index = (within[None, :] - jnp.take_along_axis(starts, source, axis=1)).astype(jnp.int32)
    return source, slot_index


def log_softmax_columns(logits):
    highest = jnp.max(logits, axis=0)
    return logits - (highest + jnp.log(jnp.sum(jnp.exp(logits - highest), axis=0)))


def reference(student_hidden, teacher_hidden, student_head, teacher_head, token_ids, requests, counts, kl_weights):
    source, slot_index = owner_layout(counts)
    owner_ids = jnp.arange(OWNERS, dtype=jnp.int32)[:, None]
    served = (requests[owner_ids, source, slot_index] + source * SERVE_DEV).astype(jnp.int32)
    teacher_rows = teacher_hidden[served.reshape(-1)]
    student_logits = jnp.dot(student_head, student_hidden.T, preferred_element_type=jnp.float32)
    teacher_logits = jnp.dot(teacher_head, teacher_rows.T, preferred_element_type=jnp.float32)
    student_log = log_softmax_columns(student_logits)
    teacher_log = log_softmax_columns(teacher_logits)
    student_prob = jnp.exp(student_log)
    gap = student_log - teacher_log
    kl = jnp.sum(student_prob * gap, axis=0)
    positions = jnp.arange(ROWS, dtype=jnp.int32)
    log_ratio = gap[token_ids, positions]
    dlogits = (kl_weights[None, :] * student_prob * (gap - kl[None, :])).astype(jnp.bfloat16)
    blocks = VOCAB // VOC_DEV
    head_blocks = student_head.reshape(blocks, VOC_DEV, D)
    grad_blocks = dlogits.reshape(blocks, VOC_DEV, ROWS)

    def accumulate(total, block_pair):
        head_block, grad_block = block_pair
        term = jnp.dot(grad_block.T, head_block, preferred_element_type=jnp.float32)
        rounded = lax.optimization_barrier(term.astype(jnp.bfloat16))
        return total + rounded.astype(jnp.float32), None

    grad_hidden, unused = lax.scan(accumulate, jnp.zeros((ROWS, D), jnp.float32), (head_blocks, grad_blocks))
    return grad_hidden, kl, log_ratio
```

```python
import functools

import jax
import jax.numpy as jnp
from jax import lax
from jax.experimental import pallas as pl
from jax.experimental.pallas import tpu as pltpu
from jax.sharding import PartitionSpec as P

MESH = pl.DeviceIdType.MESH
F32 = jnp.float32
BF16 = jnp.bfloat16


def kernel(
    spans, tiles, cores,
    counts_ref, student_ref, teacher_ref, student_head, teacher_head, token_ref, request_ref, weight_ref,
    grad_ref, row_ref,
    heads, hidden, slots, arrived, logits, stats, terms, core_in, core_out, tile_in, tile_out, span_in, span_out,
    head_sem, slot_send, slot_recv, span_send, tile_send, core_send, span_recv, tile_recv, core_recv,
    stat_send, stat_recv, gcore_send, gcore_recv, gtile_send, gtile_recv, gspan_send, gspan_recv,
):
    group = lax.axis_index("groups")
    v = lax.axis_index("vocab")
    t = lax.axis_index("tokens")
    s = lax.axis_index("sub")
    owners = tiles * cores
    members = spans * owners
    owner = t * cores + s
    me = v * owners + owner
    rows, width = student_ref.shape
    columns = student_head.shape[0]
    capacity = request_ref.shape[1] // owners

    def remote(src, dst, send, recv, at):
        copy = pltpu.make_async_remote_copy(
            src_ref=src, dst_ref=dst, send_sem=send, recv_sem=recv,
            device_id=(group,) + tuple(at), device_id_type=MESH,
        )
        copy.start()

    def drain(ref, sem):
        pltpu.make_async_copy(ref, ref, sem).wait()

    def member(index):
        return (index // owners, (index % owners) // cores, index % cores)

    def around(i):
        return lax.rem(me + i, members)

    @pl.loop(1, members)
    def _(i):
        pl.semaphore_signal(
            pltpu.get_barrier_semaphore(), inc=1, device_id=(group,) + member(around(i)), device_id_type=MESH
        )

    head_copies = [
        pltpu.make_async_copy(ref, heads.at[which], head_sem.at[which])
        for which, ref in enumerate((student_head, teacher_head))
    ]
    for copy in head_copies:
        copy.start()

    served = teacher_ref.shape[0]
    wanted = request_ref[pl.ds(owner, 1), :]
    pick = (lax.broadcasted_iota(jnp.int32, (served, owners * capacity), 0) == wanted).astype(F32).astype(BF16)
    slots[...] = (
        lax.dot_general(pick, teacher_ref[...], (((0,), (0,)), ((), ())), preferred_element_type=F32)
        .astype(BF16)
        .reshape(owners, capacity, width)
    )
    arrived[owner] = slots[owner]
    hidden[0, v, t, s] = student_ref[...]

    pl.semaphore_wait(pltpu.get_barrier_semaphore(), members - 1)

    for i in range(1, owners):
        other = lax.rem(owner + i, owners)
        remote(slots.at[other], arrived.at[owner], slot_send, slot_recv, (v, other // cores, lax.rem(other, cores)))

    def to_tiles(a, w):
        for i in range(1, tiles):
            remote(hidden.at[a, w, t, s], hidden.at[a, w, t, s], tile_send.at[a], tile_recv.at[a, w],
                   (v, lax.rem(t + i, tiles), s))

    def to_core(a, w, u):
        for i in range(1, cores):
            remote(hidden.at[a, w, u, s], hidden.at[a, w, u, s], core_send.at[a], core_recv.at[a, w],
                   (v, t, lax.rem(s + i, cores)))

    def to_spans(a):
        for d in range(1, spans):
            remote(hidden.at[a, v, t, s], hidden.at[a, v, t, s], span_send.at[a], span_recv.at[a, v],
                   (lax.rem(v + spans - d, spans), t, s))

    def start_own(a):
        to_spans(a)
        to_tiles(a, v)
        to_core(a, v, t)

    def take_teacher():
        drain(arrived.at[pl.ds(0, owners - 1)], slot_recv)
        line = lax.broadcasted_iota(jnp.int32, (rows, owners * capacity), 0)
        lane = lax.broadcasted_iota(jnp.int32, (rows, owners * capacity), 1)
        chosen = jnp.zeros((rows, owners * capacity), jnp.int32)
        start = jnp.int32(0)
        for j in range(owners):
            count = counts_ref[owner, j]
            place = lane - j * capacity
            hit = (place >= 0) & (place < count) & (place + start == line)
            chosen = jnp.where(hit, 1, chosen)
            start = start + count
        mine = jnp.dot(
            chosen.astype(F32).astype(BF16),
            arrived[...].reshape(owners * capacity, width),
            preferred_element_type=F32,
        )
        hidden[1, v, t, s] = mine.astype(BF16)
        start_own(1)

    def span_step(a, d):
        if d == 0:
            return
        w = lax.rem(v + d, spans)
        drain(hidden.at[a, w, t, s], span_recv.at[a, w])
        to_tiles(a, w)
        to_core(a, w, t)

    def tile_step(a, d):
        w = lax.rem(v + d, spans)
        if tiles > 1:
            drain(hidden.at[a, w, pl.ds(0, tiles - 1), 0], tile_recv.at[a, w])
        for i in range(1, tiles):
            to_core(a, w, lax.rem(t + i, tiles))

    def core_step(a, d):
        w = lax.rem(v + d, spans)
        if cores > 1:
            drain(hidden.at[a, w, :, pl.ds(0, cores - 1)], core_recv.at[a, w])
        if d == 0:
            head_copies[a].wait()
        part = lax.dot_general(
            heads[a, :, pl.ds(pl.multiple_of(w * width, width), width)],
            hidden[a, w].reshape(owners * rows, width),
            (((1,), (1,)), ((), ())),
            preferred_element_type=F32,
        )
        logits[a] = part if d == 0 else logits[a] + part

    start_own(0)
    units = [(0, 0)]
    for d in range(spans):
        if d + 1 < spans:
            units.append((0, d + 1))
        units.append((1, d))
    for i in range(len(units) + 2):
        if i < len(units):
            if units[i] == (1, 0):
                take_teacher()
            span_step(*units[i])
        if 0 <= i - 1 < len(units):
            tile_step(*units[i - 1])
        if 0 <= i - 2:
            core_step(*units[i - 2])

    student, teacher = logits[0], logits[1]
    ids = me * columns + lax.broadcasted_iota(jnp.int32, student.shape, 0)
    here = ids == token_ref[...]
    gap = student - teacher
    student_top = jnp.max(student, axis=0, keepdims=True)
    teacher_top = jnp.max(teacher, axis=0, keepdims=True)
    student_exp = jnp.exp(student - student_top)
    parts = [
        student_top,
        teacher_top,
        jnp.sum(student_exp, axis=0, keepdims=True),
        jnp.sum(jnp.exp(teacher - teacher_top), axis=0, keepdims=True),
        jnp.sum(student_exp * gap, axis=0, keepdims=True),
        jnp.sum(jnp.where(here, gap, 0.0), axis=0, keepdims=True),
    ]
    parts += [jnp.zeros_like(student_top)] * 2
    stats[me] = jnp.concatenate(parts, axis=0)

    @pl.loop(1, members)
    def _(i):
        remote(stats.at[me], stats.at[me], stat_send, stat_recv, member(around(i)))

    drain(stats.at[pl.ds(0, members - 1)], stat_recv)
    every = stats[...]
    student_tops, teacher_tops = every[:, 0, :], every[:, 1, :]
    top_s = jnp.max(student_tops, axis=0, keepdims=True)
    top_t = jnp.max(teacher_tops, axis=0, keepdims=True)
    scale_s = jnp.exp(student_tops - top_s)
    scale_t = jnp.exp(teacher_tops - top_t)
    total_s = jnp.sum(scale_s * every[:, 2, :], axis=0, keepdims=True)
    total_t = jnp.sum(scale_t * every[:, 3, :], axis=0, keepdims=True)
    cross = jnp.sum(scale_s * every[:, 4, :], axis=0, keepdims=True)
    hit = jnp.sum(every[:, 5, :], axis=0, keepdims=True)
    norm_s = top_s + jnp.log(total_s)
    norm_t = top_t + jnp.log(total_t)
    shift = norm_t - norm_s
    kl = cross / total_s + shift
    ratio = hit + shift
    prob = jnp.exp(logits[0] - norm_s)
    slope = (weight_ref[...] * prob * (logits[0] - logits[1] + shift - kl)).astype(BF16)

    def grad_block(d):
        w = lax.rem(v + d, spans)
        term = lax.dot_general(
            slope,
            heads[0, :, pl.ds(pl.multiple_of(w * width, width), width)],
            (((0,), (0,)), ((), ())),
            preferred_element_type=F32,
        )
        terms[d] = term.reshape(tiles, cores, rows, width)
        core_out[d] = term.astype(BF16).reshape(tiles, cores, rows, width)
        for i in range(1, cores):
            peer = lax.rem(s + i, cores)
            for u in range(tiles):
                remote(core_out.at[d, u, peer], core_in.at[d, s, u], gcore_send, gcore_recv.at[d], (v, t, peer))

    def grad_core(d):
        drain(core_in.at[d, pl.ds(0, cores - 1)], gcore_recv.at[d])
        for i in range(1, tiles + 1):
            u = lax.rem(t + i, tiles)
            total = terms[d, u, s]
            for j in range(1, cores):
                total = total + core_in[d, lax.rem(s + j, cores), u].astype(F32)
            if i < tiles:
                tile_out[d, u] = total.astype(BF16)
                remote(tile_out.at[d, u], tile_in.at[d, t], gtile_send, gtile_recv.at[d], (v, u, s))
            else:
                terms[d, u, s] = total

    def grad_tile(d):
        if tiles > 1:
            drain(tile_in.at[d, pl.ds(0, tiles - 1)], gtile_recv.at[d])
        total = terms[d, t, s]
        for i in range(1, tiles):
            total = total + tile_in[d, lax.rem(t + i, tiles)].astype(F32)
        if d == 0:
            grad_ref[...] = total
        else:
            span_out[d] = total.astype(BF16)
            remote(span_out.at[d], span_in.at[d], gspan_send, gspan_recv, (lax.rem(v + d, spans), t, s))

    order = list(range(1, spans)) + [0]
    for i in range(len(order) + 2):
        if i < len(order):
            grad_block(order[i])
        if 0 <= i - 1 < len(order):
            grad_core(order[i - 1])
        if 0 <= i - 2:
            grad_tile(order[i - 2])

    turn = lax.rem(owners - owner, owners) * rows
    row_ref[...] = pltpu.roll(
        jnp.concatenate([kl, ratio] + [jnp.zeros_like(kl)] * 6, axis=0), turn, axis=1
    )

    total = grad_ref[...]
    drain(span_in.at[pl.ds(1, spans - 1)], gspan_recv)
    for d in range(1, spans):
        total = total + span_in[d].astype(F32)
    grad_ref[...] = total

    drain(slots.at[pl.ds(0, owners - 1)], slot_send)
    for a in range(2):
        drain(hidden.at[a, pl.ds(0, spans - 1), 0, 0], span_send.at[a])
        if tiles > 1:
            drain(hidden.at[a, :, pl.ds(0, tiles - 1), 0], tile_send.at[a])
        drain(hidden.at[a, :, :, pl.ds(0, cores - 1)], core_send.at[a])
    drain(stats.at[pl.ds(0, members - 1)], stat_send)
    drain(core_out.at[:, :, pl.ds(0, cores - 1)], gcore_send)
    if tiles > 1:
        drain(tile_out.at[:, pl.ds(0, tiles - 1)], gtile_send)
    drain(span_out.at[pl.ds(1, spans - 1)], gspan_send)


def on_device(mesh, student_hidden, teacher_hidden, student_head, teacher_head, token_ids, requests, counts, kl_weights):
    spans, tiles, cores = (mesh.shape[name] for name in ("vocab", "tokens", "sub"))
    owners = tiles * cores
    members = spans * owners
    rows, width = student_hidden.shape
    columns, features = student_head.shape
    capacity = requests.shape[2]
    total_rows = owners * rows
    vmem = pl.BlockSpec(memory_space=pltpu.VMEM)
    dma = pltpu.SemaphoreType.DMA
    grad, row_values = pl.pallas_call(
        functools.partial(kernel, spans, tiles, cores),
        out_shape=(
            jax.ShapeDtypeStruct((rows, width), F32),
            jax.ShapeDtypeStruct((8, total_rows), F32),
        ),
        in_specs=[
            pl.BlockSpec(memory_space=pltpu.SMEM), vmem, vmem,
            pl.BlockSpec(memory_space=pl.ANY), pl.BlockSpec(memory_space=pl.ANY), vmem, vmem, vmem,
        ],
        out_specs=(vmem, vmem),
        scratch_shapes=[
            pltpu.VMEM((2, columns, features), BF16),
            pltpu.VMEM((2, spans, tiles, cores, rows, width), BF16),
            pltpu.VMEM((owners, capacity, width), BF16),
            pltpu.VMEM((owners, capacity, width), BF16),
            pltpu.VMEM((2, columns, total_rows), F32),
            pltpu.VMEM((members, 8, total_rows), F32),
            pltpu.VMEM((spans, tiles, cores, rows, width), F32),
            pltpu.VMEM((spans, cores, tiles, rows, width), BF16),
            pltpu.VMEM((spans, tiles, cores, rows, width), BF16),
            pltpu.VMEM((spans, tiles, rows, width), BF16),
            pltpu.VMEM((spans, tiles, rows, width), BF16),
            pltpu.VMEM((spans, rows, width), BF16),
            pltpu.VMEM((spans, rows, width), BF16),
            dma((2,)), dma, dma, dma((2,)), dma((2,)), dma((2,)),
            dma((2, spans)), dma((2, spans)), dma((2, spans)),
            dma, dma, dma, dma((spans,)), dma, dma((spans,)), dma, dma,
        ],
        compiler_params=pltpu.CompilerParams(
            collective_id=0, has_side_effects=True, vmem_limit_bytes=56 * 1024 * 1024
        ),
    )(
        counts, student_hidden, teacher_hidden, student_head, teacher_head,
        token_ids.reshape(1, total_rows),
        requests.transpose(1, 0, 2).reshape(owners, owners * capacity),
        kl_weights.reshape(1, total_rows),
    )
    return grad, row_values[0, :rows], row_values[1, :rows]


def solution(mesh):
    placed = (
        P(("groups", "tokens", "sub"), "vocab"),
        P(("groups", "tokens", "sub"), "vocab"),
        P(("vocab", "tokens", "sub"), None),
        P(("vocab", "tokens", "sub"), None),
        P("groups"),
        P("groups", None, None),
        P("groups", None),
        P("groups"),
    )
    return jax.shard_map(
        functools.partial(on_device, mesh),
        mesh=mesh,
        in_specs=placed,
        out_specs=(
            P(("groups", "tokens", "sub"), "vocab"),
            P(("groups", "tokens", "sub")),
            P(("groups", "tokens", "sub")),
        ),
        check_vma=False,
    )
```

```python
import functools

import jax
import jax.numpy as jnp
from jax import lax
from jax.experimental import pallas as pl
from jax.experimental.pallas import tpu as pltpu
from jax.sharding import PartitionSpec as P

MESH = pl.DeviceIdType.MESH
F32 = jnp.float32
BF16 = jnp.bfloat16
PIECES = 2
LATE = (2, 4, 4, 8)
CROSS = ((1, 1), (1, 3))


def kernel(
    spans, tiles, cores, pieces,
    counts_ref, student_ref, teacher_ref, student_head, teacher_head, token_ref, request_ref, weight_ref,
    grad_ref, row_ref,
    heads, hidden, slots, arrived, logits, stats, terms, core_in, core_out, tile_in, tile_out, span_in, span_out,
    head_sem, slot_send, slot_recv, span_send, cross_send, tile_send, core_send, span_recv, tile_recv, core_recv,
    stat_send, stat_recv, gcore_send, gcore_recv, gtile_send, gtile_recv, gspan_send, gspan_recv,
):
    group = lax.axis_index("groups")
    v = lax.axis_index("vocab")
    t = lax.axis_index("tokens")
    s = lax.axis_index("sub")
    owners = tiles * cores
    members = spans * owners
    owner = t * cores + s
    me = v * owners + owner
    rows, width = student_ref.shape
    columns = student_head.shape[0]
    capacity = request_ref.shape[2]

    def remote(src, dst, send, recv, at):
        copy = pltpu.make_async_remote_copy(
            src_ref=src, dst_ref=dst, send_sem=send, recv_sem=recv,
            device_id=(group,) + tuple(at), device_id_type=MESH,
        )
        copy.start()

    def drain(ref, sem):
        pltpu.make_async_copy(ref, ref, sem).wait()

    def member(index):
        return (index // owners, (index % owners) // cores, index % cores)

    def around(i):
        return lax.rem(me + i, members)

    @pl.loop(1, members, unroll=members - 1 if members <= 16 else 1)
    def _(i):
        pl.semaphore_signal(
            pltpu.get_barrier_semaphore(), inc=1, device_id=(group,) + member(around(i)), device_id_type=MESH
        )

    head_copies = [
        pltpu.make_async_copy(ref, heads.at[which], head_sem.at[which])
        for which, ref in enumerate((student_head, teacher_head))
    ]
    for copy in head_copies:
        copy.start()

    served = teacher_ref.shape[0]
    for o in range(owners):
        wanted = request_ref[o, pl.ds(owner, 1), :]
        pick = (lax.broadcasted_iota(jnp.int32, (served, capacity), 0) == wanted).astype(F32).astype(BF16)
        slots[o] = lax.dot_general(
            pick, teacher_ref[...], (((0,), (0,)), ((), ())), preferred_element_type=F32
        ).astype(BF16)
    arrived[owner] = slots[owner]
    hidden[0, v, t, s] = student_ref[...]

    pl.semaphore_wait(pltpu.get_barrier_semaphore(), members - 1)

    for i in range(1, owners):
        other = lax.rem(owner + i, owners)
        remote(slots.at[other], arrived.at[owner], slot_send, slot_recv, (v, other // cores, lax.rem(other, cores)))

    def to_tiles(a, w):
        for i in range(1, tiles):
            remote(hidden.at[a, w, t, s], hidden.at[a, w, t, s], tile_send.at[a], tile_recv.at[a, w],
                   (v, lax.rem(t + i, tiles), s))

    def to_core(a, w):
        for i in range(1, cores):
            remote(hidden.at[a, w, :, s], hidden.at[a, w, :, s], core_send.at[a], core_recv.at[a, w],
                   (v, t, lax.rem(s + i, cores)))

    def to_spans(a):
        for d in range(1, spans):
            remote(hidden.at[a, v, t, s], hidden.at[a, v, t, s], span_send.at[a], span_recv.at[a, v],
                   (lax.rem(v + spans - d, spans), t, s))

    def crosses(a, d):
        return tiles > 1 and (a, d) in CROSS

    def to_cross(a):
        for d in range(1, spans):
            if crosses(a, d):
                for i in range(1, tiles):
                    u = lax.rem(t + i, tiles)
                    remote(hidden.at[a, v, u, s], hidden.at[a, v, u, s], cross_send, tile_recv.at[a, v],
                           (lax.rem(v + spans - d, spans), t, s))

    def start_own(a):
        to_spans(a)
        to_tiles(a, v)

    def take_teacher():
        drain(arrived.at[pl.ds(0, owners - 1)], slot_recv)
        line = lax.broadcasted_iota(jnp.int32, (rows, owners * capacity), 0)
        lane = lax.broadcasted_iota(jnp.int32, (rows, owners * capacity), 1)
        chosen = jnp.zeros((rows, owners * capacity), jnp.int32)
        start = jnp.int32(0)
        for j in range(owners):
            count = counts_ref[owner, j]
            place = lane - j * capacity
            hit = (place >= 0) & (place < count) & (place + start == line)
            chosen = jnp.where(hit, 1, chosen)
            start = start + count
        mine = jnp.dot(
            chosen.astype(F32).astype(BF16),
            arrived[...].reshape(owners * capacity, width),
            preferred_element_type=F32,
        )
        hidden[1, v, t, s] = mine.astype(BF16)
        start_own(1)

    def span_step(a, d):
        if d == 0:
            return
        w = lax.rem(v + d, spans)
        drain(hidden.at[a, w, t, s], span_recv.at[a, w])
        if not crosses(a, d):
            to_tiles(a, w)

    def tile_step(a, d):
        w = lax.rem(v + d, spans)
        if tiles > 1:
            drain(hidden.at[a, w, pl.ds(0, tiles - 1), 0], tile_recv.at[a, w])
            if d == 0:
                to_cross(a)
        to_core(a, w)

    def core_step(a, d):
        w = lax.rem(v + d, spans)
        if cores > 1:
            drain(hidden.at[a, w, :, pl.ds(0, cores - 1)], core_recv.at[a, w])
        if d == 0:
            head_copies[a].wait()
        part = lax.dot_general(
            heads[a, :, pl.ds(pl.multiple_of(w * width, width), width)],
            hidden[a, w].reshape(owners * rows, width),
            (((1,), (1,)), ((), ())),
            preferred_element_type=F32,
        )
        logits[a] = part if d == 0 else logits[a] + part

    start_own(0)
    units = [(0, 0)]
    for d in range(spans):
        if d + 1 < spans:
            units.append((0, d + 1))
        units.append((1, d))
    for i in range(len(units) + LATE[1]):
        if i < len(units):
            if units[i] == (1, 0):
                take_teacher()
            span_step(*units[i])
        if 0 <= i - LATE[0] < len(units):
            tile_step(*units[i - LATE[0]])
        if 0 <= i - LATE[1]:
            core_step(*units[i - LATE[1]])

    student, teacher = logits[0], logits[1]
    ids = me * columns + lax.broadcasted_iota(jnp.int32, student.shape, 0)
    here = ids == token_ref[...]
    gap = student - teacher
    student_top = jnp.max(student, axis=0, keepdims=True)
    teacher_top = jnp.max(teacher, axis=0, keepdims=True)
    student_exp = jnp.exp(student - student_top)
    parts = [
        student_top,
        teacher_top,
        jnp.sum(student_exp, axis=0, keepdims=True),
        jnp.sum(jnp.exp(teacher - teacher_top), axis=0, keepdims=True),
        jnp.sum(student_exp * gap, axis=0, keepdims=True),
        jnp.sum(jnp.where(here, gap, 0.0), axis=0, keepdims=True),
    ]
    parts += [jnp.zeros_like(student_top)] * 2
    stats[me] = jnp.concatenate(parts, axis=0)

    @pl.loop(1, members, unroll=members - 1 if members <= 16 else 1)
    def _(i):
        remote(stats.at[me], stats.at[me], stat_send, stat_recv, member(around(i)))

    drain(stats.at[pl.ds(0, members - 1)], stat_recv)
    every = stats[...]
    student_tops, teacher_tops = every[:, 0, :], every[:, 1, :]
    top_s = jnp.max(student_tops, axis=0, keepdims=True)
    top_t = jnp.max(teacher_tops, axis=0, keepdims=True)
    scale_s = jnp.exp(student_tops - top_s)
    scale_t = jnp.exp(teacher_tops - top_t)
    total_s = jnp.sum(scale_s * every[:, 2, :], axis=0, keepdims=True)
    total_t = jnp.sum(scale_t * every[:, 3, :], axis=0, keepdims=True)
    cross = jnp.sum(scale_s * every[:, 4, :], axis=0, keepdims=True)
    hit = jnp.sum(every[:, 5, :], axis=0, keepdims=True)
    norm_s = top_s + jnp.log(total_s)
    norm_t = top_t + jnp.log(total_t)
    shift = norm_t - norm_s
    kl = cross / total_s + shift
    ratio = hit + shift
    prob = jnp.exp(logits[0] - norm_s)
    slope = (weight_ref[...] * prob * (logits[0] - logits[1] + shift - kl)).astype(BF16)

    cut = width // pieces

    def grad_block(d):
        w = lax.rem(v + d // pieces, spans)
        from_column = pl.multiple_of(w * width + d % pieces * cut, cut)
        term = lax.dot_general(
            slope,
            heads[0, :, pl.ds(from_column, cut)],
            (((0,), (0,)), ((), ())),
            preferred_element_type=F32,
        )
        terms[d] = term.reshape(tiles, cores, rows, cut)
        sent = term.astype(BF16).reshape(tiles, cores, rows, cut)
        for k in range(cores):
            core_out[d, k] = sent[:, k]
        for i in range(1, cores):
            peer = lax.rem(s + i, cores)
            remote(core_out.at[d, peer], core_in.at[d, s], gcore_send, gcore_recv.at[d], (v, t, peer))

    def grad_core(d):
        drain(core_in.at[d, pl.ds(0, cores - 1)], gcore_recv.at[d])
        for i in range(1, tiles + 1):
            u = lax.rem(t + i, tiles)
            total = terms[d, u, s]
            for j in range(1, cores):
                total = total + core_in[d, lax.rem(s + j, cores), u].astype(F32)
            if i < tiles:
                tile_out[d, u] = total.astype(BF16)
                remote(tile_out.at[d, u], tile_in.at[d, t], gtile_send, gtile_recv.at[d], (v, u, s))
            else:
                terms[d, u, s] = total

    def grad_tile(d):
        if tiles > 1:
            drain(tile_in.at[d, pl.ds(0, tiles - 1)], gtile_recv.at[d])
        total = terms[d, t, s]
        for i in range(1, tiles):
            total = total + tile_in[d, lax.rem(t + i, tiles)].astype(F32)
        if d < pieces:
            grad_ref[:, d * cut:(d + 1) * cut] = total
        else:
            span_out[d] = total.astype(BF16)
            remote(span_out.at[d], span_in.at[d], gspan_send, gspan_recv, (lax.rem(v + d // pieces, spans), t, s))

    order = list(range(pieces, spans * pieces)) + list(range(pieces))
    for i in range(len(order) + LATE[3]):
        if i < len(order):
            grad_block(order[i])
        if 0 <= i - LATE[2] < len(order):
            grad_core(order[i - LATE[2]])
        if 0 <= i - LATE[3]:
            grad_tile(order[i - LATE[3]])

    turn = lax.rem(owners - owner, owners) * rows
    row_ref[...] = pltpu.roll(
        jnp.concatenate([kl, ratio] + [jnp.zeros_like(kl)] * 6, axis=0), turn, axis=1
    )

    drain(span_in.at[pl.ds(pieces, (spans - 1) * pieces)], gspan_recv)
    for h in range(pieces):
        total = grad_ref[:, h * cut:(h + 1) * cut]
        for d in range(1, spans):
            total = total + span_in[d * pieces + h].astype(F32)
        grad_ref[:, h * cut:(h + 1) * cut] = total

    drain(slots.at[pl.ds(0, owners - 1)], slot_send)
    for a in range(2):
        drain(hidden.at[a, pl.ds(0, spans - 1), 0, 0], span_send.at[a])
        if tiles > 1:
            direct = sum(not crosses(a, d) for d in range(spans))
            drain(hidden.at[a, pl.ds(0, direct), pl.ds(0, tiles - 1), 0], tile_send.at[a])
        drain(hidden.at[a, :, :, pl.ds(0, cores - 1)], core_send.at[a])
    crossed = sum(crosses(a, d) for a in range(2) for d in range(1, spans))
    if crossed:
        drain(hidden.at[0, pl.ds(0, crossed), pl.ds(0, tiles - 1), 0], cross_send)
    drain(stats.at[pl.ds(0, members - 1)], stat_send)
    drain(core_out.at[:, pl.ds(0, cores - 1)], gcore_send)
    if tiles > 1:
        drain(tile_out.at[:, pl.ds(0, tiles - 1)], gtile_send)
    drain(span_out.at[pl.ds(pieces, (spans - 1) * pieces)], gspan_send)


def on_device(mesh, student_hidden, teacher_hidden, student_head, teacher_head, token_ids, requests, counts, kl_weights):
    spans, tiles, cores = (mesh.shape[name] for name in ("vocab", "tokens", "sub"))
    owners = tiles * cores
    members = spans * owners
    rows, width = student_hidden.shape
    columns, features = student_head.shape
    capacity = requests.shape[2]
    total_rows = owners * rows
    pieces = PIECES if width % (128 * PIECES) == 0 else 1
    vmem = pl.BlockSpec(memory_space=pltpu.VMEM)
    dma = pltpu.SemaphoreType.DMA
    grad, row_values = pl.pallas_call(
        functools.partial(kernel, spans, tiles, cores, pieces),
        out_shape=(
            jax.ShapeDtypeStruct((rows, width), F32),
            jax.ShapeDtypeStruct((8, total_rows), F32),
        ),
        in_specs=[
            pl.BlockSpec(memory_space=pltpu.SMEM), vmem, vmem,
            pl.BlockSpec(memory_space=pl.ANY), pl.BlockSpec(memory_space=pl.ANY), vmem, vmem, vmem,
        ],
        out_specs=(vmem, vmem),
        scratch_shapes=[
            pltpu.VMEM((2, columns, features), BF16),
            pltpu.VMEM((2, spans, tiles, cores, rows, width), BF16),
            pltpu.VMEM((owners, capacity, width), BF16),
            pltpu.VMEM((owners, capacity, width), BF16),
            pltpu.VMEM((2, columns, total_rows), F32),
            pltpu.VMEM((members, 8, total_rows), F32),
            pltpu.VMEM((spans * pieces, tiles, cores, rows, width // pieces), F32),
            pltpu.VMEM((spans * pieces, cores, tiles, rows, width // pieces), BF16),
            pltpu.VMEM((spans * pieces, cores, tiles, rows, width // pieces), BF16),
            pltpu.VMEM((spans * pieces, tiles, rows, width // pieces), BF16),
            pltpu.VMEM((spans * pieces, tiles, rows, width // pieces), BF16),
            pltpu.VMEM((spans * pieces, rows, width // pieces), BF16),
            pltpu.VMEM((spans * pieces, rows, width // pieces), BF16),
            dma((2,)), dma, dma, dma((2,)), dma, dma((2,)), dma((2,)),
            dma((2, spans)), dma((2, spans)), dma((2, spans)),
            dma, dma, dma, dma((spans * pieces,)), dma, dma((spans * pieces,)), dma, dma,
        ],
        compiler_params=pltpu.CompilerParams(
            collective_id=0, has_side_effects=True, vmem_limit_bytes=56 * 1024 * 1024
        ),
    )(
        counts, student_hidden, teacher_hidden, student_head, teacher_head,
        token_ids.reshape(1, total_rows),
        requests,
        kl_weights.reshape(1, total_rows),
    )
    return grad, row_values[0, :rows], row_values[1, :rows]


def solution(mesh):
    placed = (
        P(("groups", "tokens", "sub"), "vocab"),
        P(("groups", "tokens", "sub"), "vocab"),
        P(("vocab", "tokens", "sub"), None),
        P(("vocab", "tokens", "sub"), None),
        P("groups"),
        P("groups", None, None),
        P("groups", None),
        P("groups"),
    )
    return jax.shard_map(
        functools.partial(on_device, mesh),
        mesh=mesh,
        in_specs=placed,
        out_specs=(
            P(("groups", "tokens", "sub"), "vocab"),
            P(("groups", "tokens", "sub")),
            P(("groups", "tokens", "sub")),
        ),
        check_vma=False,
    )
```

```python
import functools

import jax
import jax.numpy as jnp
from jax import lax
from jax.experimental import pallas as pl
from jax.experimental.pallas import tpu as pltpu
from jax.sharding import PartitionSpec as P

MESH = pl.DeviceIdType.MESH
F32 = jnp.float32
BF16 = jnp.bfloat16
PIECES = 2
LATE = (2, 4, 4, 8)
CROSS = ((1, 1), (1, 3))


def kernel(
    spans, tiles, cores, pieces,
    counts_ref, student_ref, teacher_ref, student_head, teacher_head, token_ref, request_ref, weight_ref,
    grad_ref, row_ref,
    heads, hidden, slots, arrived, logits, stats, terms, core_in, core_out, tile_in, tile_out, span_in, span_out,
    head_sem, slot_send, slot_recv, span_send, cross_send, tile_send, core_send, span_recv, tile_recv, core_recv,
    stat_send, stat_recv, gcore_send, gcore_recv, gtile_send, gtile_recv, gspan_send, gspan_recv,
):
    group = lax.axis_index("groups")
    v = lax.axis_index("vocab")
    t = lax.axis_index("tokens")
    s = lax.axis_index("sub")
    owners = tiles * cores
    members = spans * owners
    owner = t * cores + s
    me = v * owners + owner
    rows, width = student_ref.shape
    columns = student_head.shape[0]
    capacity = request_ref.shape[2]

    def remote(src, dst, send, recv, at):
        copy = pltpu.make_async_remote_copy(
            src_ref=src, dst_ref=dst, send_sem=send, recv_sem=recv,
            device_id=(group,) + tuple(at), device_id_type=MESH,
        )
        copy.start()

    def drain(ref, sem):
        pltpu.make_async_copy(ref, ref, sem).wait()

    def member(index):
        return (index // owners, (index % owners) // cores, index % cores)

    def around(i):
        return lax.rem(me + i, members)

    @pl.loop(1, members, unroll=members - 1 if members <= 16 else 1)
    def _(i):
        pl.semaphore_signal(
            pltpu.get_barrier_semaphore(), inc=1, device_id=(group,) + member(around(i)), device_id_type=MESH
        )

    head_copies = [
        pltpu.make_async_copy(ref, heads.at[which], head_sem.at[which])
        for which, ref in enumerate((student_head, teacher_head))
    ]
    for copy in head_copies:
        copy.start()

    served = teacher_ref.shape[0]
    for o in range(owners):
        wanted = request_ref[o, pl.ds(owner, 1), :]
        pick = (lax.broadcasted_iota(jnp.int32, (served, capacity), 0) == wanted).astype(F32).astype(BF16)
        slots[o] = lax.dot_general(
            pick, teacher_ref[...], (((0,), (0,)), ((), ())), preferred_element_type=F32
        ).astype(BF16)
    arrived[owner] = slots[owner]
    hidden[0, v, t, s] = student_ref[...]

    pl.semaphore_wait(pltpu.get_barrier_semaphore(), members - 1)

    for i in range(1, owners):
        other = lax.rem(owner + i, owners)
        remote(slots.at[other], arrived.at[owner], slot_send, slot_recv, (v, other // cores, lax.rem(other, cores)))

    def to_tiles(a, w):
        for i in range(1, tiles):
            remote(hidden.at[a, w, t, s], hidden.at[a, w, t, s], tile_send.at[a], tile_recv.at[a, w],
                   (v, lax.rem(t + i, tiles), s))

    def to_core(a, w):
        for i in range(1, cores):
            remote(hidden.at[a, w, :, s], hidden.at[a, w, :, s], core_send.at[a], core_recv.at[a, w],
                   (v, t, lax.rem(s + i, cores)))

    def to_spans(a):
        for d in range(1, spans):
            remote(hidden.at[a, v, t, s], hidden.at[a, v, t, s], span_send.at[a], span_recv.at[a, v],
                   (lax.rem(v + spans - d, spans), t, s))

    def crosses(a, d):
        return tiles > 1 and (a, d) in CROSS

    def to_cross(a):
        for d in range(1, spans):
            if crosses(a, d):
                for i in range(1, tiles):
                    u = lax.rem(t + i, tiles)
                    remote(hidden.at[a, v, u, s], hidden.at[a, v, u, s], cross_send, tile_recv.at[a, v],
                           (lax.rem(v + spans - d, spans), t, s))

    def start_own(a):
        to_tiles(a, v)
        to_spans(a)

    def take_teacher():
        drain(arrived.at[pl.ds(0, owners - 1)], slot_recv)
        line = lax.broadcasted_iota(jnp.int32, (rows, owners * capacity), 0)
        lane = lax.broadcasted_iota(jnp.int32, (rows, owners * capacity), 1)
        chosen = jnp.zeros((rows, owners * capacity), jnp.int32)
        start = jnp.int32(0)
        for j in range(owners):
            count = counts_ref[owner, j]
            place = lane - j * capacity
            hit = (place >= 0) & (place < count) & (place + start == line)
            chosen = jnp.where(hit, 1, chosen)
            start = start + count
        mine = jnp.dot(
            chosen.astype(F32).astype(BF16),
            arrived[...].reshape(owners * capacity, width),
            preferred_element_type=F32,
        )
        hidden[1, v, t, s] = mine.astype(BF16)
        start_own(1)

    def span_step(a, d):
        if d == 0:
            return
        w = lax.rem(v + d, spans)
        drain(hidden.at[a, w, t, s], span_recv.at[a, w])
        if not crosses(a, d):
            to_tiles(a, w)

    def tile_step(a, d):
        w = lax.rem(v + d, spans)
        if tiles > 1:
            drain(hidden.at[a, w, pl.ds(0, tiles - 1), 0], tile_recv.at[a, w])
            if d == 0:
                to_cross(a)
        to_core(a, w)

    def core_step(a, d):
        w = lax.rem(v + d, spans)
        if cores > 1:
            drain(hidden.at[a, w, :, pl.ds(0, cores - 1)], core_recv.at[a, w])
        if d == 0:
            head_copies[a].wait()
        part = lax.dot_general(
            heads[a, :, pl.ds(pl.multiple_of(w * width, width), width)],
            hidden[a, w].reshape(owners * rows, width),
            (((1,), (1,)), ((), ())),
            preferred_element_type=F32,
        )
        logits[a] = part if d == 0 else logits[a] + part

    start_own(0)
    units = [(0, 0)]
    for d in range(spans):
        if d + 1 < spans:
            units.append((0, d + 1))
        units.append((1, d))
    for i in range(len(units) + LATE[1]):
        if i < len(units):
            if units[i] == (1, 0):
                take_teacher()
            span_step(*units[i])
        if 0 <= i - LATE[0] < len(units):
            tile_step(*units[i - LATE[0]])
        if 0 <= i - LATE[1]:
            core_step(*units[i - LATE[1]])

    student, teacher = logits[0], logits[1]
    ids = me * columns + lax.broadcasted_iota(jnp.int32, student.shape, 0)
    here = ids == token_ref[...]
    gap = student - teacher
    student_top = jnp.max(student, axis=0, keepdims=True)
    teacher_top = jnp.max(teacher, axis=0, keepdims=True)
    student_exp = jnp.exp(student - student_top)
    parts = [
        student_top,
        teacher_top,
        jnp.sum(student_exp, axis=0, keepdims=True),
        jnp.sum(jnp.exp(teacher - teacher_top), axis=0, keepdims=True),
        jnp.sum(student_exp * gap, axis=0, keepdims=True),
        jnp.sum(jnp.where(here, gap, 0.0), axis=0, keepdims=True),
    ]
    parts += [jnp.zeros_like(student_top)] * 2
    stats[me] = jnp.concatenate(parts, axis=0)

    @pl.loop(1, members, unroll=members - 1 if members <= 16 else 1)
    def _(i):
        remote(stats.at[me], stats.at[me], stat_send, stat_recv, member(around(i)))

    drain(stats.at[pl.ds(0, members - 1)], stat_recv)
    every = stats[...]
    student_tops, teacher_tops = every[:, 0, :], every[:, 1, :]
    top_s = jnp.max(student_tops, axis=0, keepdims=True)
    top_t = jnp.max(teacher_tops, axis=0, keepdims=True)
    scale_s = jnp.exp(student_tops - top_s)
    scale_t = jnp.exp(teacher_tops - top_t)
    total_s = jnp.sum(scale_s * every[:, 2, :], axis=0, keepdims=True)
    total_t = jnp.sum(scale_t * every[:, 3, :], axis=0, keepdims=True)
    cross = jnp.sum(scale_s * every[:, 4, :], axis=0, keepdims=True)
    hit = jnp.sum(every[:, 5, :], axis=0, keepdims=True)
    norm_s = top_s + jnp.log(total_s)
    norm_t = top_t + jnp.log(total_t)
    shift = norm_t - norm_s
    kl = cross / total_s + shift
    ratio = hit + shift
    prob = jnp.exp(logits[0] - norm_s)
    slope = (weight_ref[...] * prob * (logits[0] - logits[1] + shift - kl)).astype(BF16)

    cut = width // pieces

    def grad_block(d):
        w = lax.rem(v + d // pieces, spans)
        from_column = pl.multiple_of(w * width + d % pieces * cut, cut)
        term = lax.dot_general(
            slope,
            heads[0, :, pl.ds(from_column, cut)],
            (((0,), (0,)), ((), ())),
            preferred_element_type=F32,
        )
        terms[d] = term.reshape(tiles, cores, rows, cut)
        sent = term.astype(BF16).reshape(tiles, cores, rows, cut)
        for k in range(cores):
            core_out[d, k] = sent[:, k]
        for i in range(1, cores):
            peer = lax.rem(s + i, cores)
            remote(core_out.at[d, peer], core_in.at[d, s], gcore_send, gcore_recv.at[d], (v, t, peer))

    def grad_core(d):
        drain(core_in.at[d, pl.ds(0, cores - 1)], gcore_recv.at[d])
        for i in range(1, tiles + 1):
            u = lax.rem(t + i, tiles)
            total = terms[d, u, s]
            for j in range(1, cores):
                total = total + core_in[d, lax.rem(s + j, cores), u].astype(F32)
            if i < tiles:
                tile_out[d, u] = total.astype(BF16)
                remote(tile_out.at[d, u], tile_in.at[d, t], gtile_send, gtile_recv.at[d], (v, u, s))
            else:
                terms[d, u, s] = total

    def grad_tile(d):
        if tiles > 1:
            drain(tile_in.at[d, pl.ds(0, tiles - 1)], gtile_recv.at[d])
        total = terms[d, t, s]
        for i in range(1, tiles):
            total = total + tile_in[d, lax.rem(t + i, tiles)].astype(F32)
        if d < pieces:
            grad_ref[:, d * cut:(d + 1) * cut] = total
        else:
            span_out[d] = total.astype(BF16)
            remote(span_out.at[d], span_in.at[d], gspan_send, gspan_recv, (lax.rem(v + d // pieces, spans), t, s))

    order = list(range(pieces, spans * pieces)) + list(range(pieces))
    for i in range(len(order) + LATE[3]):
        if i < len(order):
            grad_block(order[i])
        if 0 <= i - LATE[2] < len(order):
            grad_core(order[i - LATE[2]])
        if 0 <= i - LATE[3]:
            grad_tile(order[i - LATE[3]])

    turn = lax.rem(owners - owner, owners) * rows
    row_ref[...] = pltpu.roll(
        jnp.concatenate([kl, ratio] + [jnp.zeros_like(kl)] * 6, axis=0), turn, axis=1
    )

    drain(span_in.at[pl.ds(pieces, (spans - 1) * pieces)], gspan_recv)
    for h in range(pieces):
        total = grad_ref[:, h * cut:(h + 1) * cut]
        for d in range(1, spans):
            total = total + span_in[d * pieces + h].astype(F32)
        grad_ref[:, h * cut:(h + 1) * cut] = total

    drain(slots.at[pl.ds(0, owners - 1)], slot_send)
    for a in range(2):
        drain(hidden.at[a, pl.ds(0, spans - 1), 0, 0], span_send.at[a])
        if tiles > 1:
            direct = sum(not crosses(a, d) for d in range(spans))
            drain(hidden.at[a, pl.ds(0, direct), pl.ds(0, tiles - 1), 0], tile_send.at[a])
        drain(hidden.at[a, :, :, pl.ds(0, cores - 1)], core_send.at[a])
    crossed = sum(crosses(a, d) for a in range(2) for d in range(1, spans))
    if crossed:
        drain(hidden.at[0, pl.ds(0, crossed), pl.ds(0, tiles - 1), 0], cross_send)
    drain(stats.at[pl.ds(0, members - 1)], stat_send)
    drain(core_out.at[:, pl.ds(0, cores - 1)], gcore_send)
    if tiles > 1:
        drain(tile_out.at[:, pl.ds(0, tiles - 1)], gtile_send)
    drain(span_out.at[pl.ds(pieces, (spans - 1) * pieces)], gspan_send)


def hand_out(grad_in, row_in, grad_ref, kl_ref, ratio_ref):
    rows = kl_ref.shape[1]
    grad_ref[...] = grad_in[...]
    kl_ref[...] = row_in[0:1, :rows]
    ratio_ref[...] = row_in[1:2, :rows]


def on_device(mesh, student_hidden, teacher_hidden, student_head, teacher_head, token_ids, requests, counts, kl_weights):
    spans, tiles, cores = (mesh.shape[name] for name in ("vocab", "tokens", "sub"))
    owners = tiles * cores
    members = spans * owners
    rows, width = student_hidden.shape
    columns, features = student_head.shape
    capacity = requests.shape[2]
    total_rows = owners * rows
    pieces = PIECES if width % (128 * PIECES) == 0 else 1
    vmem = pl.BlockSpec(memory_space=pltpu.VMEM)
    dma = pltpu.SemaphoreType.DMA
    grad, row_values = pl.pallas_call(
        functools.partial(kernel, spans, tiles, cores, pieces),
        out_shape=(
            jax.ShapeDtypeStruct((rows, width), F32),
            jax.ShapeDtypeStruct((8, total_rows), F32),
        ),
        in_specs=[
            pl.BlockSpec(memory_space=pltpu.SMEM), vmem, vmem,
            pl.BlockSpec(memory_space=pl.ANY), pl.BlockSpec(memory_space=pl.ANY), vmem, vmem, vmem,
        ],
        out_specs=(vmem, vmem),
        scratch_shapes=[
            pltpu.VMEM((2, columns, features), BF16),
            pltpu.VMEM((2, spans, tiles, cores, rows, width), BF16),
            pltpu.VMEM((owners, capacity, width), BF16),
            pltpu.VMEM((owners, capacity, width), BF16),
            pltpu.VMEM((2, columns, total_rows), F32),
            pltpu.VMEM((members, 8, total_rows), F32),
            pltpu.VMEM((spans * pieces, tiles, cores, rows, width // pieces), F32),
            pltpu.VMEM((spans * pieces, cores, tiles, rows, width // pieces), BF16),
            pltpu.VMEM((spans * pieces, cores, tiles, rows, width // pieces), BF16),
            pltpu.VMEM((spans * pieces, tiles, rows, width // pieces), BF16),
            pltpu.VMEM((spans * pieces, tiles, rows, width // pieces), BF16),
            pltpu.VMEM((spans * pieces, rows, width // pieces), BF16),
            pltpu.VMEM((spans * pieces, rows, width // pieces), BF16),
            dma((2,)), dma, dma, dma((2,)), dma, dma((2,)), dma((2,)),
            dma((2, spans)), dma((2, spans)), dma((2, spans)),
            dma, dma, dma, dma((spans * pieces,)), dma, dma((spans * pieces,)), dma, dma,
        ],
        compiler_params=pltpu.CompilerParams(
            collective_id=0, has_side_effects=True, vmem_limit_bytes=56 * 1024 * 1024
        ),
    )(
        counts, student_hidden, teacher_hidden, student_head, teacher_head,
        token_ids.reshape(1, total_rows),
        requests,
        kl_weights.reshape(1, total_rows),
    )
    grad, kl, log_ratio = pl.pallas_call(
        hand_out,
        out_shape=(
            jax.ShapeDtypeStruct((rows, width), F32),
            jax.ShapeDtypeStruct((1, rows), F32),
            jax.ShapeDtypeStruct((1, rows), F32),
        ),
        in_specs=[vmem, vmem],
        out_specs=(vmem, vmem, vmem),
    )(grad, row_values)
    return grad, kl.reshape(rows), log_ratio.reshape(rows)


def solution(mesh):
    placed = (
        P(("groups", "tokens", "sub"), "vocab"),
        P(("groups", "tokens", "sub"), "vocab"),
        P(("vocab", "tokens", "sub"), None),
        P(("vocab", "tokens", "sub"), None),
        P("groups"),
        P("groups", None, None),
        P("groups", None),
        P("groups"),
    )
    return jax.shard_map(
        functools.partial(on_device, mesh),
        mesh=mesh,
        in_specs=placed,
        out_specs=(
            P(("groups", "tokens", "sub"), "vocab"),
            P(("groups", "tokens", "sub")),
            P(("groups", "tokens", "sub")),
        ),
        check_vma=False,
    )
```

```python
import functools

import jax
import jax.numpy as jnp
from jax import lax
from jax.experimental import pallas as pl
from jax.experimental.pallas import tpu as pltpu
from jax.sharding import PartitionSpec as P

MESH = pl.DeviceIdType.MESH
F32 = jnp.float32
BF16 = jnp.bfloat16
PIECES = 2
LATE = (2, 4, 4, 8)
CROSS = ((1, 2), (1, 3))


def kernel(
    spans, tiles, cores, pieces,
    counts_ref, student_ref, teacher_ref, student_head, teacher_head, token_ref, request_ref, weight_ref,
    grad_ref, row_ref,
    heads, hidden, slots, arrived, logits, stats, terms, core_in, core_out, tile_in, tile_out, span_in, span_out,
    head_sem, slot_send, slot_recv, span_send, cross_send, tile_send, core_send, span_recv, tile_recv, core_recv,
    stat_send, stat_recv, gcore_send, gcore_recv, gtile_send, gtile_recv, gspan_send, gspan_recv,
):
    group = lax.axis_index("groups")
    v = lax.axis_index("vocab")
    t = lax.axis_index("tokens")
    s = lax.axis_index("sub")
    owners = tiles * cores
    members = spans * owners
    owner = t * cores + s
    me = v * owners + owner
    rows, width = student_ref.shape
    columns = student_head.shape[0]
    capacity = request_ref.shape[2]

    def remote(src, dst, send, recv, at):
        copy = pltpu.make_async_remote_copy(
            src_ref=src, dst_ref=dst, send_sem=send, recv_sem=recv,
            device_id=(group,) + tuple(at), device_id_type=MESH,
        )
        copy.start()

    def drain(ref, sem):
        pltpu.make_async_copy(ref, ref, sem).wait()

    def member(index):
        return (index // owners, (index % owners) // cores, index % cores)

    def around(i):
        return lax.rem(me + i, members)

    @pl.loop(1, members, unroll=members - 1 if members <= 16 else 1)
    def _(i):
        pl.semaphore_signal(
            pltpu.get_barrier_semaphore(), inc=1, device_id=(group,) + member(around(i)), device_id_type=MESH
        )

    head_copies = [
        pltpu.make_async_copy(ref, heads.at[which], head_sem.at[which])
        for which, ref in enumerate((student_head, teacher_head))
    ]
    for copy in head_copies:
        copy.start()

    served = teacher_ref.shape[0]
    for o in range(owners):
        wanted = request_ref[o, pl.ds(owner, 1), :]
        pick = (lax.broadcasted_iota(jnp.int32, (served, capacity), 0) == wanted).astype(F32).astype(BF16)
        slots[o] = lax.dot_general(
            pick, teacher_ref[...], (((0,), (0,)), ((), ())), preferred_element_type=F32
        ).astype(BF16)
    arrived[owner] = slots[owner]
    hidden[0, v, t, s] = student_ref[...]

    pl.semaphore_wait(pltpu.get_barrier_semaphore(), members - 1)

    for i in range(1, owners):
        other = lax.rem(owner + i, owners)
        remote(slots.at[other], arrived.at[owner], slot_send, slot_recv, (v, other // cores, lax.rem(other, cores)))

    def to_tiles(a, w):
        for i in range(1, tiles):
            remote(hidden.at[a, w, t, s], hidden.at[a, w, t, s], tile_send.at[a], tile_recv.at[a, w],
                   (v, lax.rem(t + i, tiles), s))

    def to_core(a, w):
        for i in range(1, cores):
            remote(hidden.at[a, w, :, s], hidden.at[a, w, :, s], core_send.at[a], core_recv.at[a, w],
                   (v, t, lax.rem(s + i, cores)))

    def to_spans(a):
        for d in range(1, spans):
            remote(hidden.at[a, v, t, s], hidden.at[a, v, t, s], span_send.at[a], span_recv.at[a, v],
                   (lax.rem(v + spans - d, spans), t, s))

    def crosses(a, d):
        return tiles > 1 and (a, d) in CROSS

    def to_cross(a):
        for d in range(1, spans):
            if crosses(a, d):
                for i in range(1, tiles):
                    u = lax.rem(t + i, tiles)
                    remote(hidden.at[a, v, u, s], hidden.at[a, v, u, s], cross_send, tile_recv.at[a, v],
                           (lax.rem(v + spans - d, spans), t, s))

    def start_own(a):
        to_tiles(a, v)
        to_spans(a)

    def take_teacher():
        drain(arrived.at[pl.ds(0, owners - 1)], slot_recv)
        line = lax.broadcasted_iota(jnp.int32, (rows, owners * capacity), 0)
        lane = lax.broadcasted_iota(jnp.int32, (rows, owners * capacity), 1)
        chosen = jnp.zeros((rows, owners * capacity), jnp.int32)
        start = jnp.int32(0)
        for j in range(owners):
            count = counts_ref[owner, j]
            place = lane - j * capacity
            hit = (place >= 0) & (place < count) & (place + start == line)
            chosen = jnp.where(hit, 1, chosen)
            start = start + count
        mine = jnp.dot(
            chosen.astype(F32).astype(BF16),
            arrived[...].reshape(owners * capacity, width),
            preferred_element_type=F32,
        )
        hidden[1, v, t, s] = mine.astype(BF16)
        start_own(1)

    def span_step(a, d):
        if d == 0:
            return
        w = lax.rem(v + d, spans)
        drain(hidden.at[a, w, t, s], span_recv.at[a, w])
        if not crosses(a, d):
            to_tiles(a, w)

    def tile_step(a, d):
        w = lax.rem(v + d, spans)
        if tiles > 1:
            drain(hidden.at[a, w, pl.ds(0, tiles - 1), 0], tile_recv.at[a, w])
            if d == 0:
                to_cross(a)
        to_core(a, w)

    def core_step(a, d):
        w = lax.rem(v + d, spans)
        if cores > 1:
            drain(hidden.at[a, w, :, pl.ds(0, cores - 1)], core_recv.at[a, w])
        if d == 0:
            head_copies[a].wait()
        part = lax.dot_general(
            heads[a, :, pl.ds(pl.multiple_of(w * width, width), width)],
            hidden[a, w].reshape(owners * rows, width),
            (((1,), (1,)), ((), ())),
            preferred_element_type=F32,
        )
        logits[a] = part if d == 0 else logits[a] + part

    start_own(0)
    units = [(0, 0)]
    for d in range(spans):
        if d + 1 < spans:
            units.append((0, d + 1))
        units.append((1, d))
    for i in range(len(units) + LATE[1]):
        if i < len(units):
            if units[i] == (1, 0):
                take_teacher()
            span_step(*units[i])
        if 0 <= i - LATE[0] < len(units):
            tile_step(*units[i - LATE[0]])
        if 0 <= i - LATE[1]:
            core_step(*units[i - LATE[1]])

    student, teacher = logits[0], logits[1]
    ids = me * columns + lax.broadcasted_iota(jnp.int32, student.shape, 0)
    here = ids == token_ref[...]
    gap = student - teacher
    student_top = jnp.max(student, axis=0, keepdims=True)
    teacher_top = jnp.max(teacher, axis=0, keepdims=True)
    student_exp = jnp.exp(student - student_top)
    parts = [
        student_top,
        teacher_top,
        jnp.sum(student_exp, axis=0, keepdims=True),
        jnp.sum(jnp.exp(teacher - teacher_top), axis=0, keepdims=True),
        jnp.sum(student_exp * gap, axis=0, keepdims=True),
        jnp.sum(jnp.where(here, gap, 0.0), axis=0, keepdims=True),
    ]
    parts += [jnp.zeros_like(student_top)] * 2
    stats[me] = jnp.concatenate(parts, axis=0)

    @pl.loop(1, members, unroll=members - 1 if members <= 16 else 1)
    def _(i):
        remote(stats.at[me], stats.at[me], stat_send, stat_recv, member(around(i)))

    drain(stats.at[pl.ds(0, members - 1)], stat_recv)
    every = stats[...]
    student_tops, teacher_tops = every[:, 0, :], every[:, 1, :]
    top_s = jnp.max(student_tops, axis=0, keepdims=True)
    top_t = jnp.max(teacher_tops, axis=0, keepdims=True)
    scale_s = jnp.exp(student_tops - top_s)
    scale_t = jnp.exp(teacher_tops - top_t)
    total_s = jnp.sum(scale_s * every[:, 2, :], axis=0, keepdims=True)
    total_t = jnp.sum(scale_t * every[:, 3, :], axis=0, keepdims=True)
    cross = jnp.sum(scale_s * every[:, 4, :], axis=0, keepdims=True)
    hit = jnp.sum(every[:, 5, :], axis=0, keepdims=True)
    norm_s = top_s + jnp.log(total_s)
    norm_t = top_t + jnp.log(total_t)
    shift = norm_t - norm_s
    kl = cross / total_s + shift
    ratio = hit + shift
    prob = jnp.exp(logits[0] - norm_s)
    slope = (weight_ref[...] * prob * (logits[0] - logits[1] + shift - kl)).astype(BF16)

    cut = width // pieces

    def grad_block(d):
        w = lax.rem(v + d // pieces, spans)
        from_column = pl.multiple_of(w * width + d % pieces * cut, cut)
        term = lax.dot_general(
            slope,
            heads[0, :, pl.ds(from_column, cut)],
            (((0,), (0,)), ((), ())),
            preferred_element_type=F32,
        )
        terms[d] = term.reshape(tiles, cores, rows, cut)
        sent = term.astype(BF16).reshape(tiles, cores, rows, cut)
        for k in range(cores):
            core_out[d, k] = sent[:, k]
        for i in range(1, cores):
            peer = lax.rem(s + i, cores)
            remote(core_out.at[d, peer], core_in.at[d, s], gcore_send, gcore_recv.at[d], (v, t, peer))

    def grad_core(d):
        drain(core_in.at[d, pl.ds(0, cores - 1)], gcore_recv.at[d])
        for i in range(1, tiles + 1):
            u = lax.rem(t + i, tiles)
            total = terms[d, u, s]
            for j in range(1, cores):
                total = total + core_in[d, lax.rem(s + j, cores), u].astype(F32)
            if i < tiles:
                tile_out[d, u] = total.astype(BF16)
                remote(tile_out.at[d, u], tile_in.at[d, t], gtile_send, gtile_recv.at[d], (v, u, s))
            else:
                terms[d, u, s] = total

    def grad_tile(d):
        if tiles > 1:
            drain(tile_in.at[d, pl.ds(0, tiles - 1)], gtile_recv.at[d])
        total = terms[d, t, s]
        for i in range(1, tiles):
            total = total + tile_in[d, lax.rem(t + i, tiles)].astype(F32)
        if d < pieces:
            grad_ref[:, d * cut:(d + 1) * cut] = total
        else:
            span_out[d] = total.astype(BF16)
            remote(span_out.at[d], span_in.at[d], gspan_send, gspan_recv, (lax.rem(v + d // pieces, spans), t, s))

    order = list(range(pieces, spans * pieces)) + list(range(pieces))
    for i in range(len(order) + LATE[3]):
        if i < len(order):
            grad_block(order[i])
        if 0 <= i - LATE[2] < len(order):
            grad_core(order[i - LATE[2]])
        if 0 <= i - LATE[3]:
            grad_tile(order[i - LATE[3]])

    turn = lax.rem(owners - owner, owners) * rows
    row_ref[...] = pltpu.roll(
        jnp.concatenate([kl, ratio] + [jnp.zeros_like(kl)] * 6, axis=0), turn, axis=1
    )

    drain(span_in.at[pl.ds(pieces, (spans - 1) * pieces)], gspan_recv)
    for h in range(pieces):
        total = grad_ref[:, h * cut:(h + 1) * cut]
        for d in range(1, spans):
            total = total + span_in[d * pieces + h].astype(F32)
        grad_ref[:, h * cut:(h + 1) * cut] = total

    drain(slots.at[pl.ds(0, owners - 1)], slot_send)
    for a in range(2):
        drain(hidden.at[a, pl.ds(0, spans - 1), 0, 0], span_send.at[a])
        if tiles > 1:
            direct = sum(not crosses(a, d) for d in range(spans))
            drain(hidden.at[a, pl.ds(0, direct), pl.ds(0, tiles - 1), 0], tile_send.at[a])
        drain(hidden.at[a, :, :, pl.ds(0, cores - 1)], core_send.at[a])
    crossed = sum(crosses(a, d) for a in range(2) for d in range(1, spans))
    if crossed:
        drain(hidden.at[0, pl.ds(0, crossed), pl.ds(0, tiles - 1), 0], cross_send)
    drain(stats.at[pl.ds(0, members - 1)], stat_send)
    drain(core_out.at[:, pl.ds(0, cores - 1)], gcore_send)
    if tiles > 1:
        drain(tile_out.at[:, pl.ds(0, tiles - 1)], gtile_send)
    drain(span_out.at[pl.ds(pieces, (spans - 1) * pieces)], gspan_send)


def hand_out(grad_in, row_in, grad_ref, kl_ref, ratio_ref):
    rows = kl_ref.shape[1]
    grad_ref[...] = grad_in[...]
    kl_ref[...] = row_in[0:1, :rows]
    ratio_ref[...] = row_in[1:2, :rows]


def on_device(mesh, student_hidden, teacher_hidden, student_head, teacher_head, token_ids, requests, counts, kl_weights):
    spans, tiles, cores = (mesh.shape[name] for name in ("vocab", "tokens", "sub"))
    owners = tiles * cores
    members = spans * owners
    rows, width = student_hidden.shape
    columns, features = student_head.shape
    capacity = requests.shape[2]
    total_rows = owners * rows
    pieces = PIECES if width % (128 * PIECES) == 0 else 1
    vmem = pl.BlockSpec(memory_space=pltpu.VMEM)
    dma = pltpu.SemaphoreType.DMA
    grad, row_values = pl.pallas_call(
        functools.partial(kernel, spans, tiles, cores, pieces),
        out_shape=(
            jax.ShapeDtypeStruct((rows, width), F32),
            jax.ShapeDtypeStruct((8, total_rows), F32),
        ),
        in_specs=[
            pl.BlockSpec(memory_space=pltpu.SMEM), vmem, vmem,
            pl.BlockSpec(memory_space=pl.ANY), pl.BlockSpec(memory_space=pl.ANY), vmem, vmem, vmem,
        ],
        out_specs=(vmem, vmem),
        scratch_shapes=[
            pltpu.VMEM((2, columns, features), BF16),
            pltpu.VMEM((2, spans, tiles, cores, rows, width), BF16),
            pltpu.VMEM((owners, capacity, width), BF16),
            pltpu.VMEM((owners, capacity, width), BF16),
            pltpu.VMEM((2, columns, total_rows), F32),
            pltpu.VMEM((members, 8, total_rows), F32),
            pltpu.VMEM((spans * pieces, tiles, cores, rows, width // pieces), F32),
            pltpu.VMEM((spans * pieces, cores, tiles, rows, width // pieces), BF16),
            pltpu.VMEM((spans * pieces, cores, tiles, rows, width // pieces), BF16),
            pltpu.VMEM((spans * pieces, tiles, rows, width // pieces), BF16),
            pltpu.VMEM((spans * pieces, tiles, rows, width // pieces), BF16),
            pltpu.VMEM((spans * pieces, rows, width // pieces), BF16),
            pltpu.VMEM((spans * pieces, rows, width // pieces), BF16),
            dma((2,)), dma, dma, dma((2,)), dma, dma((2,)), dma((2,)),
            dma((2, spans)), dma((2, spans)), dma((2, spans)),
            dma, dma, dma, dma((spans * pieces,)), dma, dma((spans * pieces,)), dma, dma,
        ],
        compiler_params=pltpu.CompilerParams(
            collective_id=0, has_side_effects=True, vmem_limit_bytes=56 * 1024 * 1024
        ),
    )(
        counts, student_hidden, teacher_hidden, student_head, teacher_head,
        token_ids.reshape(1, total_rows),
        requests,
        kl_weights.reshape(1, total_rows),
    )
    grad, kl, log_ratio = pl.pallas_call(
        hand_out,
        out_shape=(
            jax.ShapeDtypeStruct((rows, width), F32),
            jax.ShapeDtypeStruct((1, rows), F32),
            jax.ShapeDtypeStruct((1, rows), F32),
        ),
        in_specs=[vmem, vmem],
        out_specs=(vmem, vmem, vmem),
    )(grad, row_values)
    return grad, kl.reshape(rows), log_ratio.reshape(rows)


def solution(mesh):
    placed = (
        P(("groups", "tokens", "sub"), "vocab"),
        P(("groups", "tokens", "sub"), "vocab"),
        P(("vocab", "tokens", "sub"), None),
        P(("vocab", "tokens", "sub"), None),
        P("groups"),
        P("groups", None, None),
        P("groups", None),
        P("groups"),
    )
    return jax.shard_map(
        functools.partial(on_device, mesh),
        mesh=mesh,
        in_specs=placed,
        out_specs=(
            P(("groups", "tokens", "sub"), "vocab"),
            P(("groups", "tokens", "sub")),
            P(("groups", "tokens", "sub")),
        ),
        check_vma=False,
    )
```
